32 devices in a mesh: groups: 2 (over x), pool: 8 (over z, y), head: 2 (over core).
Axes of the slice: x: 2, y: 2, z: 4, core: 2. Of those that a mesh axis runs over, the one named last changes fastest.
Arguments:
- queries: bfloat16 [2048, 32, 128], P(('groups', 'pool'), 'head'), parts along dimension 0, may hold values from -400 to 400
- new_kv: bfloat16 [2048, 2, 4, 128], P(('groups', 'pool'), None, 'head'), parts along dimension 0, may hold values from -4 to 4
- pool: bfloat16 [528, 2, 4, 128, 128], P(('groups', 'pool'), None, 'head'), parts along dimension 0, may hold values from -6 to 6
- block_table: int32 [8, 64], P('groups'), parts along dimension 0, may hold values from -1 to 263, as said below
- prefix_len: int32 [8], P('groups'), parts along dimension 0, may hold values from 2048 to 8192, as said below
- new_slots: int32 [16], P('groups'), parts along dimension 0, may hold values from 0 to 263, as said below
Outputs:
- attended: bfloat16 [2048, 32, 128], P(('groups', 'pool'), 'head'), parts along dimension 0
- updated_pool: bfloat16 [528, 2, 4, 128, 128], P(('groups', 'pool'), None, 'head'), parts along dimension 0
The draws below stay inside these ranges and needn't reach their ends.
There are 2 independent parts, one for each index of `groups`. The reference program is written for one: setup_inputs(seed, part) draws one part's arguments, and reference() takes and returns one part's arrays. A program takes and returns all parts, laid end to end along the dimension named above; each array names one. Nothing has to cross between parts.
Inputs may be any that keep to these rules, and one draw needn't show every extreme that they name: `block_table`: entry [r, j] is the slot (owner times 33 plus local slot) of page j of request r for j < ceil(prefix_len[r] / 128), and -1 after. All named slots differ. No owner holds more than 8 pages of one request, and the request with the longest prefix has exactly 8 on every owner. `prefix_len`: the longest prefix is exactly 8192 tokens. `new_slots`: entry d is a slot of owner d (d * 33 to (d + 1) * 33 - 1) that block_table does not name.
All inputs are finite; a program needn't handle non-finite values.
Results may differ from the reference program's by a relative error of at most 0.012.
Values may be sent and summed in bfloat16 or wider, within the bound.
A program may use at most 128 MiB of HBM per device.

```python
import jax
import jax.numpy as jnp
from jax import lax

HD = 128
KVH = 4
GQ = 8
PAGE = 128
PMAX = 64
QH = 32
NEWTOK = 256
OWNERS = 8
REQS = 4
TOKENS = 1024
SLOTS = 33


def layout(key):
    folded = jax.random.fold_in(key, 7)
    subkeys = jax.random.split(folded, 5)
    lengths = jax.random.randint(subkeys[0], (REQS,), PMAX * PAGE // 4, PMAX * PAGE + 1)
    longest = jax.random.randint(subkeys[1], (), 0, REQS)
    request = jnp.arange(REQS)
    lengths = jnp.where(request == longest, PMAX * PAGE, lengths).astype(jnp.int32)
    page_count = (lengths + PAGE - 1) // PAGE
    starts = jnp.cumsum(page_count) - page_count
    used_total = jnp.sum(page_count)
    column = jnp.arange(PMAX)
    page_order = starts[:, None] + column[None, :]
    offset_owner = jax.random.randint(subkeys[2], (), 0, OWNERS)
    owner_perm = jax.random.permutation(subkeys[3], OWNERS)
    slot_perm = jax.random.permutation(subkeys[4], SLOTS)

    def placed(index):
        return owner_perm[(index + offset_owner) % OWNERS] * SLOTS + slot_perm[jnp.minimum(index // OWNERS, SLOTS - 1)]
    block_rows = jnp.where(column[None, :] < page_count[:, None], placed(page_order), -1).astype(jnp.int32)
    owner_ids = jnp.arange(OWNERS)
    inverse = jnp.argsort(owner_perm)
    rank = (inverse[owner_ids] - offset_owner) % OWNERS
    used_here = used_total // OWNERS + (rank < used_total % OWNERS).astype(jnp.int32)
    fresh = owner_ids * SLOTS + slot_perm[jnp.minimum(used_here, SLOTS - 1)]
    return (block_rows, lengths, fresh.astype(jnp.int32))


def token_draw(key):
    folded = jax.random.fold_in(key, 11)
    subkeys = jax.random.split(folded, 2)
    query_vals = jax.random.truncated_normal(subkeys[0], -4.0, 4.0, (TOKENS, QH, HD), jnp.float32)
    pair_vals = jax.random.truncated_normal(subkeys[1], -4.0, 4.0, (TOKENS, 2, KVH, HD), jnp.float32)
    return (query_vals, pair_vals)


def draw_queries(key, part):
    return token_draw(key)[0].astype(jnp.bfloat16)


def draw_new_kv(key, part):
    return token_draw(key)[1].astype(jnp.bfloat16)


def draw_block_table(key, part):
    return layout(key)[0]


def draw_prefix_len(key, part):
    return layout(key)[1]


def draw_new_slots(key, part):
    return layout(key)[2]


def block_scale(key, extent, pieces, least, top_value):
    loudness = 1.0
    for axis_at, blocks in pieces:
        steps = jax.random.uniform(jax.random.fold_in(jax.random.fold_in(key, 6), axis_at), (blocks,), jnp.float32, least / len(pieces), top_value / len(pieces))
        loudness = loudness * jnp.repeat(jnp.exp(steps), extent[axis_at] // blocks).reshape((-1,) + (1,) * (len(extent) - 1 - axis_at))
    return loudness


def normal_values(stream_key, dims, width, reach, shards=(), held_as=jnp.bfloat16):
    gain = block_scale(stream_key, dims, shards, -0.22, 0.18) if shards else 1.0
    drawn = jax.random.normal(stream_key, dims, jnp.float32) * width * gain
    return jnp.minimum(jnp.maximum(drawn, -reach), reach).astype(held_as)


def setup_inputs(seed: int = 0, part: int = 0) -> dict:
    arg_keys = jax.random.split(jax.random.key(seed), 7)
    own_keys = jax.random.split(jax.random.fold_in(arg_keys[6], part), 7)
    queries = draw_queries(jax.random.fold_in(jax.random.fold_in(arg_keys[6], part), 71), part)
    new_kv = draw_new_kv(jax.random.fold_in(jax.random.fold_in(arg_keys[6], part), 71), part)
    pool = normal_values(own_keys[2], (OWNERS * SLOTS, 2, KVH, PAGE, HD), 1.0, 6.0, ((0, 8), (2, 2)))
    block_table = draw_block_table(jax.random.fold_in(jax.random.fold_in(arg_keys[6], part), 71), part)
    prefix_len = draw_prefix_len(jax.random.fold_in(jax.random.fold_in(arg_keys[6], part), 71), part)
    new_slots = draw_new_slots(jax.random.fold_in(jax.random.fold_in(arg_keys[6], part), 71), part)
    return {"queries": queries, "new_kv": new_kv, "pool": pool, "block_table": block_table, "prefix_len": prefix_len, "new_slots": new_slots}


neg_big = -1e30


def one_request(request_id, queries, new_kv, pool, block_table, prefix_len):
    slot_ids = jnp.maximum(block_table[request_id], 0)
    pages = pool[slot_ids]
    prefix_keys = pages[:, 0].transpose(1, 0, 2, 3).reshape(KVH, PMAX * PAGE, HD)
    prefix_vals = pages[:, 1].transpose(1, 0, 2, 3).reshape(KVH, PMAX * PAGE, HD)
    start = (request_id * NEWTOK).astype(jnp.int32)
    swapped = ((1 - request_id % 2) * PAGE).astype(jnp.int32)
    recent = jnp.roll(lax.dynamic_slice_in_dim(new_kv, start, NEWTOK, 0), swapped, axis=0)
    all_keys = jnp.concatenate([prefix_keys, recent[:, 0].transpose(1, 0, 2)], axis=1)
    all_vals = jnp.concatenate([prefix_vals, recent[:, 1].transpose(1, 0, 2)], axis=1)
    query_block = jnp.roll(lax.dynamic_slice_in_dim(queries, start, NEWTOK, 0), swapped, axis=0).reshape(NEWTOK, KVH, GQ, HD)
    scores = jnp.einsum("tkgd,knd->kgtn", query_block.astype(jnp.float32), all_keys.astype(jnp.float32)) * HD ** -0.5
    position = jnp.arange(PMAX * PAGE, dtype=jnp.int32)
    prefix_mask = jnp.broadcast_to(position[None, :] < prefix_len[request_id], (NEWTOK, PMAX * PAGE))
    token_pos = jnp.arange(NEWTOK, dtype=jnp.int32)
    causal = token_pos[None, :] <= token_pos[:, None]
    allowed = jnp.concatenate([prefix_mask, causal], axis=1)[None, None]
    scores = jnp.where(allowed, scores, neg_big)
    row_max = jnp.max(scores, axis=-1, keepdims=True)
    weights = jnp.where(allowed, jnp.exp(scores - row_max), 0.0)
    row_total = jnp.sum(weights, axis=-1)
    rounded = weights.astype(jnp.bfloat16).astype(jnp.float32)
    mixed = jnp.einsum("kgtn,knd->kgtd", rounded, all_vals.astype(jnp.float32)) / row_total[..., None]
    logical = mixed.transpose(2, 0, 1, 3).reshape(NEWTOK, QH, HD).astype(jnp.bfloat16)
    return jnp.roll(logical, swapped, axis=0)


def reference(queries, new_kv, pool, block_table, prefix_len, new_slots):
    outputs = lax.map(lambda request_id: one_request(request_id, queries, new_kv, pool, block_table, prefix_len), jnp.arange(REQS, dtype=jnp.int32))
    attended = outputs.reshape(TOKENS, QH, HD)
    new_pages = new_kv.reshape(2 * REQS, PAGE, 2, KVH, HD).transpose(0, 2, 3, 1, 4)
    updated_pool = pool.at[new_slots].set(new_pages)
    return attended, updated_pool
```

```python
import functools
import math

import jax
import jax.numpy as jnp
import numpy as np
from jax import lax
from jax.experimental import pallas as pl
from jax.experimental.pallas import tpu as pltpu
from jax.sharding import PartitionSpec as P

neg_big = -1e30
vmem_bytes = 32 * 1024 * 1024


def permuted(array, apart):
    return lax.ppermute(array, "pool", [(i, i ^ apart) for i in range(lax.axis_size("pool"))])


def half_of(ids):
    return 1 - (ids % 2 ^ ids // 2 % 2)


def select_pages(rows, page_count, holder, first_rank, take, slot_count):
    width = rows.shape[1]
    column = jnp.arange(width, dtype=jnp.int32)
    owned = (
        (rows >= holder[:, None] * slot_count)
        & (rows < (holder[:, None] + 1) * slot_count)
        & (column[None, :] < page_count[:, None])
    )
    before = column[None, :, None] > column[None, None, :]
    rank = jnp.sum((owned[:, None, :] & before).astype(jnp.int32), axis=-1)
    wanted = first_rank[:, None] + 2 * jnp.arange(take, dtype=jnp.int32)[None, :]
    matched = owned[:, None, :] & (rank[:, None, :] == wanted[:, :, None])
    present = jnp.any(matched, axis=-1)
    chosen = jnp.sum(jnp.where(matched, column[None, None, :], 0), axis=-1)
    local = rows - holder[:, None] * slot_count
    slot_id = jnp.sum(jnp.where(matched, local[:, None, :], 0), axis=-1)
    return chosen, slot_id, present


def gather_kernel(slots_ref, pool_ref, out_ref, sems):
    for i in range(out_ref.shape[0]):
        pltpu.make_async_copy(pool_ref.at[slots_ref[i]], out_ref.at[i], sems.at[i]).start()
    for i in range(out_ref.shape[0]):
        pltpu.make_async_copy(pool_ref.at[slots_ref[i]], out_ref.at[i], sems.at[i]).wait()


def gather_pages(pool, slots):
    count = slots.shape[0]
    return pl.pallas_call(
        gather_kernel,
        out_shape=jax.ShapeDtypeStruct((count, *pool.shape[1:]), pool.dtype),
        in_specs=[pl.BlockSpec(memory_space=pltpu.SMEM), pl.BlockSpec(memory_space=pl.ANY)],
        out_specs=pl.BlockSpec(memory_space=pl.ANY),
        scratch_shapes=[pltpu.SemaphoreType.DMA((count,))],
        name="gather_pages",
    )(slots, pool)


def attend_kernel(with_recent, chunk, group, valid_ref, *refs):
    if with_recent:
        q_a, q_b, pages, recent = refs[:4]
        refs = refs[4:]
    else:
        q_a, q_b, pages = refs[:3]
        refs = refs[3:]
    o_a, o_b, lse_a, lse_b, m_ref, l_ref, acc_ref = refs
    n_pages, _, _, page_len, head_dim = pages.shape
    rows = q_a.shape[1]
    factor = head_dim ** (-0.5) * math.log2(math.e)
    sides = (q_a, q_b)
    m_ref[...] = jnp.full_like(m_ref, neg_big)
    l_ref[...] = jnp.zeros_like(l_ref)
    acc_ref[...] = jnp.zeros_like(acc_ref)

    def step(keys, values, masks):
        scores = [
            lax.dot_general(
                keys, q[0], (((1,), (1,)), ((), ())), preferred_element_type=jnp.float32
            )
            for q in sides
        ]
        for side in range(2):
            s = scores[side]
            if masks is not None:
                s = jnp.where(masks[side], s, 2 * neg_big)
            m_old = m_ref[side]
            m_new = jnp.maximum(m_old, jnp.max(s, axis=0, keepdims=True))
            p = jnp.exp2((s - m_new) * factor)
            alpha = jnp.exp2((m_old - m_new) * factor)
            m_ref[side] = m_new
            l_ref[side] = l_ref[side] * alpha + jnp.sum(p, axis=0, keepdims=True)
            acc_ref[side] = acc_ref[side] * alpha + lax.dot_general(
                values,
                p.astype(jnp.bfloat16),
                (((0,), (0,)), ((), ())),
                preferred_element_type=jnp.float32,
            )

    key_at = lax.broadcasted_iota(jnp.int32, (page_len, rows), 0)
    for begin in range(0, n_pages, chunk):
        counts = [valid_ref[begin + i] for i in range(chunk)]
        least = functools.reduce(jnp.minimum, counts)

        @pl.when(least == page_len)
        def whole():
            span = pl.ds(begin, chunk)
            step(
                pages[span, 0, 0].reshape(chunk * page_len, head_dim),
                pages[span, 1, 0].reshape(chunk * page_len, head_dim),
                None,
            )

        @pl.when(least < page_len)
        def parts():
            for i in range(chunk):

                @pl.when(counts[i] > 0)
                def part():
                    seen = key_at < counts[i]
                    step(pages[begin + i, 0, 0], pages[begin + i, 1, 0], (seen, seen))

    if with_recent:
        token = lax.broadcasted_iota(jnp.int32, (page_len, rows), 1) + pl.program_id(1) * rows
        own_seen = key_at * group <= token
        other_seen = key_at < valid_ref[n_pages]
        step(recent[0, 0, 0], recent[0, 1, 0], (own_seen, other_seen))

    for side, (o_ref, lse_ref) in enumerate(((o_a, lse_a), (o_b, lse_b))):
        total = jnp.maximum(l_ref[side], 1e-30)
        o_ref[0] = (acc_ref[side] / total).astype(o_ref.dtype)
        lse_ref[0] = m_ref[side] * factor + jnp.log2(total)


def attend(valid, q_a, q_b, pages, recent, group):
    kv_heads, n_rows, head_dim = q_a.shape
    n_pages, _, _, page_len, _ = pages.shape
    rows = math.gcd(n_rows, 256)
    chunk = math.gcd(n_pages, 4)
    q_spec = pl.BlockSpec((1, rows, head_dim), lambda k, b: (k, b, 0))
    page_block = lambda count: pl.BlockSpec(
        (count, 2, 1, page_len, head_dim), lambda k, b: (0, 0, k, 0, 0)
    )
    o_spec = pl.BlockSpec((1, head_dim, rows), lambda k, b: (k, 0, b))
    lse_spec = pl.BlockSpec((1, 1, rows), lambda k, b: (k, 0, b))
    o_shape = jax.ShapeDtypeStruct((kv_heads, head_dim, n_rows), jnp.bfloat16)
    lse_shape = jax.ShapeDtypeStruct((kv_heads, 1, n_rows), jnp.float32)
    operands = (valid, q_a, q_b, pages) + (() if recent is None else (recent,))
    work = kv_heads * 2 * n_rows * n_pages * page_len
    return pl.pallas_call(
        functools.partial(attend_kernel, recent is not None, chunk, group),
        grid=(kv_heads, n_rows // rows),
        out_shape=(o_shape, o_shape, lse_shape, lse_shape),
        in_specs=[pl.BlockSpec(memory_space=pltpu.SMEM), q_spec, q_spec, page_block(n_pages)]
        + ([] if recent is None else [page_block(1)]),
        out_specs=(o_spec, o_spec, lse_spec, lse_spec),
        scratch_shapes=[
            pltpu.VMEM((2, 1, rows), jnp.float32),
            pltpu.VMEM((2, 1, rows), jnp.float32),
            pltpu.VMEM((2, head_dim, rows), jnp.float32),
        ],
        compiler_params=pltpu.CompilerParams(vmem_limit_bytes=vmem_bytes),
        cost_estimate=pl.CostEstimate(
            flops=4 * work * head_dim, bytes_accessed=6 * 2**20, transcendentals=work
        ),
        name="attend_far" if recent is None else "attend_near",
    )(*operands)


def combine(parts):
    top = functools.reduce(jnp.maximum, [lse for _, lse in parts])
    weights = [jnp.exp2(lse - top) for _, lse in parts]
    total = functools.reduce(jnp.add, weights)
    mixed = functools.reduce(
        jnp.add, [o.astype(jnp.float32) * w for (o, _), w in zip(parts, weights)]
    )
    return mixed / total, top + jnp.log2(total)


def merge_kernel(group, *refs):
    out_ref = refs[-1]
    parts = [(refs[2 * i], refs[2 * i + 1]) for i in range(len(refs) // 2)]
    tokens = out_ref.shape[0]
    heads = []
    for k in range(parts[0][0].shape[0]):
        mixed, _ = combine([(o[k], lse[k]) for o, lse in parts])
        heads.append(mixed.T.reshape(tokens, group, mixed.shape[0]))
    out_ref[...] = jnp.concatenate(heads, axis=1).astype(out_ref.dtype)


def on_device(queries, new_kv, pool, block_table, prefix_len, new_slots):
    owners = lax.axis_size("pool")
    half_count = owners // 2
    me = lax.axis_index("pool")
    slot_count, _, kv_heads, page_len, head_dim = pool.shape
    tokens, q_heads, _ = queries.shape
    group = q_heads // kv_heads
    take = block_table.shape[1] // owners // 2
    n_pages = half_count * take
    my_half = me // half_count
    far_half = 1 - my_half

    q_own = queries.reshape(tokens, kv_heads, group, head_dim).transpose(1, 0, 2, 3)
    q_own = q_own.reshape(kv_heads, tokens * group, head_dim)
    q_far = permuted(q_own, half_count)
    q_pair = permuted(q_own, 1)
    q_far_pair = permuted(q_far, 1)

    page_count = (prefix_len + page_len - 1) // page_len
    targets = np.arange(owners, dtype=np.int32)
    first = jnp.asarray(half_of(targets))
    _, send_slots, _ = select_pages(
        jnp.repeat(block_table, 2, axis=0),
        jnp.repeat(page_count, 2, axis=0),
        jnp.full((owners,), me, jnp.int32),
        first,
        take,
        slot_count,
    )
    groups = [list(range(half_count)), list(range(half_count, owners))]

    def exchange(which):
        slots = lax.dynamic_slice_in_dim(send_slots, which * half_count, half_count, 0)
        sent = gather_pages(pool, slots.reshape(-1))
        return lax.all_to_all(
            sent, "pool", split_axis=0, concat_axis=0, tiled=True, axis_index_groups=groups
        )

    pages_far = exchange(far_half)
    pages_near = exchange(my_half)

    holders = my_half * half_count + jnp.arange(half_count, dtype=jnp.int32)

    def valid_keys(device):
        row = lax.dynamic_slice_in_dim(block_table, device // 2, 1, 0)
        length = lax.dynamic_slice_in_dim(prefix_len, device // 2, 1, 0)
        chosen, _, present = select_pages(
            jnp.broadcast_to(row, (half_count, row.shape[1])),
            jnp.broadcast_to((length + page_len - 1) // page_len, (half_count,)),
            holders,
            jnp.broadcast_to(half_of(device), (half_count,)),
            take,
            slot_count,
        )
        left = jnp.clip(length[:, None] - chosen * page_len, 0, page_len)
        return jnp.where(present, left, 0).reshape(-1)

    valid_far = valid_keys(me ^ half_count)
    other_limit = ((1 - half_of(me)) * page_len).reshape(1).astype(jnp.int32)
    valid_near = jnp.concatenate([valid_keys(me), other_limit])

    new_page = new_kv.transpose(1, 2, 0, 3)[None]
    o_far, o_far_pair, lse_far, lse_far_pair = attend(
        valid_far, q_far, q_far_pair, pages_far, None, group
    )
    back_o, back_lse = permuted(o_far_pair, 1), permuted(lse_far_pair, 1)
    far_o, far_lse = combine([(o_far, lse_far), (back_o, back_lse)])
    home_o = permuted(far_o.astype(jnp.bfloat16), half_count)
    home_lse = permuted(far_lse, half_count)

    o_near, o_pair, lse_near, lse_pair = attend(
        valid_near, q_own, q_pair, pages_near, new_page, group
    )
    pair_o, pair_lse = permuted(o_pair, 1), permuted(lse_pair, 1)
    attended = pl.pallas_call(
        functools.partial(merge_kernel, group),
        out_shape=jax.ShapeDtypeStruct(queries.shape, queries.dtype),
        compiler_params=pltpu.CompilerParams(vmem_limit_bytes=vmem_bytes),
        name="merge",
    )(o_near, lse_near, pair_o, pair_lse, home_o, home_lse)

    own_slot = lax.dynamic_index_in_dim(new_slots, me, 0, keepdims=False)
    updated_pool = lax.dynamic_update_slice_in_dim(pool, new_page, own_slot % slot_count, 0)
    return attended, updated_pool


def solution(mesh):
    placed = (
        P(("groups", "pool"), "head", None),
        P(("groups", "pool"), None, "head", None),
        P(("groups", "pool"), None, "head", None, None),
        P("groups", None),
        P("groups"),
        P("groups"),
    )
    return jax.shard_map(
        on_device,
        mesh=mesh,
        in_specs=placed,
        out_specs=(
            P(("groups", "pool"), "head", None),
            P(("groups", "pool"), None, "head", None, None),
        ),
        check_vma=False,
    )
```

```python
import functools
import math

import jax
import jax.numpy as jnp
import numpy as np
from jax import lax
from jax.experimental import pallas as pl
from jax.experimental.pallas import tpu as pltpu
from jax.sharding import PartitionSpec as P

neg_big = -1e30
vmem_bytes = 32 * 1024 * 1024
lanes = 128
block_rows = 1024
sub_rows = 256
chunk_pages = 16


def permuted(array, apart):
    return lax.ppermute(array, "pool", [(i, i ^ apart) for i in range(lax.axis_size("pool"))])


def half_of(ids):
    return 1 - (ids % 2 ^ ids // 2 % 2)


def select_pages(rows, page_count, holder, first_rank, take, slot_count):
    width = rows.shape[1]
    column = jnp.arange(width, dtype=jnp.int32)
    owned = (
        (rows >= holder[:, None] * slot_count)
        & (rows < (holder[:, None] + 1) * slot_count)
        & (column[None, :] < page_count[:, None])
    )
    before = column[None, :, None] > column[None, None, :]
    rank = jnp.sum((owned[:, None, :] & before).astype(jnp.int32), axis=-1)
    wanted = first_rank[:, None] + 2 * jnp.arange(take, dtype=jnp.int32)[None, :]
    matched = owned[:, None, :] & (rank[:, None, :] == wanted[:, :, None])
    present = jnp.any(matched, axis=-1)
    chosen = jnp.sum(jnp.where(matched, column[None, None, :], 0), axis=-1)
    local = rows - holder[:, None] * slot_count
    slot_id = jnp.sum(jnp.where(matched, local[:, None, :], 0), axis=-1)
    return chosen, slot_id, present


def gather_kernel(slots_ref, pool_ref, out_ref, sems):
    for i in range(out_ref.shape[0]):
        pltpu.make_async_copy(pool_ref.at[slots_ref[i]], out_ref.at[i], sems.at[i]).start()
    for i in range(out_ref.shape[0]):
        pltpu.make_async_copy(pool_ref.at[slots_ref[i]], out_ref.at[i], sems.at[i]).wait()


def gather_pages(pool, slots):
    count = slots.shape[0]
    return pl.pallas_call(
        gather_kernel,
        out_shape=jax.ShapeDtypeStruct((count, *pool.shape[1:]), pool.dtype),
        in_specs=[pl.BlockSpec(memory_space=pltpu.SMEM), pl.BlockSpec(memory_space=pl.ANY)],
        out_specs=pl.BlockSpec(memory_space=pltpu.VMEM),
        scratch_shapes=[pltpu.SemaphoreType.DMA((count,))],
        compiler_params=pltpu.CompilerParams(vmem_limit_bytes=vmem_bytes),
        cost_estimate=pl.CostEstimate(
            flops=0, bytes_accessed=2 * count * pool.nbytes // pool.shape[0], transcendentals=0
        ),
        name="gather_pages",
    )(slots, pool)


def attend_kernel(with_recent, chunk, group, valid_ref, bias_ref, q_ref, pages, *refs):
    if with_recent:
        recent, refs = refs[0], refs[1:]
    o_ref, lse_ref, m_ref, l_ref, acc_ref = refs
    n_pages, _, _, page_len, head_dim = pages.shape
    rows = q_ref.shape[1]
    factor = head_dim ** (-0.5) * math.log2(math.e)
    m_ref[...] = jnp.full_like(m_ref, neg_big)
    l_ref[...] = jnp.zeros_like(l_ref)
    acc_ref[...] = jnp.zeros_like(acc_ref)

    def step(keys, values, mask):
        parts = max(rows // sub_rows, 1)
        size = rows // parts
        for part in range(parts):
            at = pl.ds(part * size, size)
            s = lax.dot_general(
                q_ref[0, at], keys, (((1,), (1,)), ((), ())), preferred_element_type=jnp.float32
            )
            s = mask(s, part * size)
            m_old = m_ref[at]
            m_new = jnp.maximum(m_old, jnp.max(s, axis=1, keepdims=True))
            alpha = jnp.exp2((m_old - m_new) * factor)
            top = m_new[:, :1]
            p = jnp.exp2((s - top) * factor)
            sums = functools.reduce(
                jnp.add,
                [p[:, i : i + lanes] for i in range(0, p.shape[1], lanes)],
            )
            m_ref[at] = m_new
            l_ref[at] = l_ref[at] * alpha + sums
            acc_ref[at] = acc_ref[at] * alpha[:, :1] + jnp.dot(
                p.astype(jnp.bfloat16), values, preferred_element_type=jnp.float32
            )

    for begin in range(0, n_pages, chunk):
        counts = [valid_ref[begin + i] for i in range(chunk)]
        least = functools.reduce(jnp.minimum, counts)
        most = functools.reduce(jnp.maximum, counts)
        span = pl.ds(begin, chunk)
        keys = pages.at[span, 0, 0]
        values = pages.at[span, 1, 0]
        shape = (chunk * page_len, head_dim)

        @pl.when(least == page_len)
        def whole():
            step(keys[...].reshape(shape), values[...].reshape(shape), lambda s, start: s)

        @pl.when((least < page_len) & (most > 0))
        def partly():
            offset = bias_ref[:, pl.ds(begin * page_len, chunk * page_len)]
            step(keys[...].reshape(shape), values[...].reshape(shape), lambda s, start: s + offset)

    if with_recent:
        limit = valid_ref[n_pages]
        causal = valid_ref[n_pages + 1]

        def seen(s, start):
            key_at = lax.broadcasted_iota(jnp.int32, s.shape, 1)
            row_at = lax.broadcasted_iota(jnp.int32, s.shape, 0)
            row_at = row_at + (pl.program_id(1) * rows + start)
            return jnp.where(
                (key_at < limit) & (key_at * group * causal <= row_at), s, 2 * neg_big
            )

        step(recent[0, 0, 0], recent[0, 1, 0], seen)

    total = jnp.maximum(jnp.sum(l_ref[...], axis=1, keepdims=True), 1e-30)
    o_ref[0] = (acc_ref[...] / total).T.astype(o_ref.dtype)
    lse = m_ref[...] * factor + jnp.log2(total)
    lse_ref[0] = lse.T[:1]


def attend(valid, q, pages, recent, group, name):
    kv_heads, n_rows, head_dim = q.shape
    n_pages, _, _, page_len, _ = pages.shape
    rows = math.gcd(n_rows, block_rows)
    chunk = math.gcd(n_pages, chunk_pages)
    page_block = lambda count: pl.BlockSpec(
        (count, 2, 1, page_len, head_dim), lambda k, b: (0, 0, k, 0, 0)
    )
    seen = jnp.arange(page_len)[None, :] < valid[:n_pages, None]
    bias = jnp.where(seen, 0.0, 2 * neg_big).astype(jnp.float32).reshape(1, n_pages * page_len)
    operands = (valid, bias, q, pages) + (() if recent is None else (recent,))
    work = kv_heads * n_rows * n_pages * page_len
    return pl.pallas_call(
        functools.partial(attend_kernel, recent is not None, chunk, group),
        grid=(kv_heads, n_rows // rows),
        out_shape=(
            jax.ShapeDtypeStruct((kv_heads, head_dim, n_rows), jnp.bfloat16),
            jax.ShapeDtypeStruct((kv_heads, 1, n_rows), jnp.float32),
        ),
        in_specs=[
            pl.BlockSpec(memory_space=pltpu.SMEM),
            pl.BlockSpec(bias.shape, lambda k, b: (0, 0)),
            pl.BlockSpec((1, rows, head_dim), lambda k, b: (k, b, 0)),
            page_block(n_pages),
        ]
        + ([] if recent is None else [page_block(1)]),
        out_specs=(
            pl.BlockSpec((1, head_dim, rows), lambda k, b: (k, 0, b)),
            pl.BlockSpec((1, 1, rows), lambda k, b: (k, 0, b)),
        ),
        scratch_shapes=[
            pltpu.VMEM((rows, lanes), jnp.float32),
            pltpu.VMEM((rows, lanes), jnp.float32),
            pltpu.VMEM((rows, head_dim), jnp.float32),
        ],
        compiler_params=pltpu.CompilerParams(vmem_limit_bytes=vmem_bytes),
        cost_estimate=pl.CostEstimate(
            flops=4 * work * head_dim, bytes_accessed=4 * 2**20, transcendentals=work
        ),
        name=name,
    )(*operands)


def write_kernel(slot_ref, pool_ref, page_ref, out_ref):
    out_ref[...] = pool_ref[...]
    count = out_ref.shape[0]
    at = slot_ref[0] - pl.program_id(0) * count
    for i in range(count):

        @pl.when(at == i)
        def put():
            out_ref[i] = page_ref[0]


def write_page(pool, page, slot):
    slot_count = pool.shape[0]
    count = max(i for i in range(1, 5) if slot_count % i == 0)
    block = (count, *pool.shape[1:])
    return pl.pallas_call(
        write_kernel,
        grid=(slot_count // count,),
        out_shape=jax.ShapeDtypeStruct(pool.shape, pool.dtype),
        in_specs=[
            pl.BlockSpec(memory_space=pltpu.SMEM),
            pl.BlockSpec(block, lambda i: (i, 0, 0, 0, 0)),
            pl.BlockSpec(page.shape, lambda i: (0, 0, 0, 0, 0)),
        ],
        out_specs=pl.BlockSpec(block, lambda i: (i, 0, 0, 0, 0)),
        compiler_params=pltpu.CompilerParams(vmem_limit_bytes=vmem_bytes),
        cost_estimate=pl.CostEstimate(flops=0, bytes_accessed=2 * pool.nbytes, transcendentals=0),
        name="write_page",
    )(slot, pool, page)


def combine(parts):
    top = functools.reduce(jnp.maximum, [lse for _, lse in parts])
    weights = [jnp.exp2(lse - top) for _, lse in parts]
    total = functools.reduce(jnp.add, weights)
    mixed = functools.reduce(
        jnp.add, [o.astype(jnp.float32) * w for (o, _), w in zip(parts, weights)]
    )
    return mixed / total, top + jnp.log2(total)


def merge_kernel(group, *refs):
    out_ref = refs[-1]
    parts = [(refs[2 * i], refs[2 * i + 1]) for i in range(len(refs) // 2)]
    tokens = out_ref.shape[0]
    heads = []
    for k in range(parts[0][0].shape[0]):
        mixed, _ = combine([(o[k], lse[k]) for o, lse in parts])
        heads.append(mixed.T.reshape(tokens, group, mixed.shape[0]))
    out_ref[...] = jnp.concatenate(heads, axis=1).astype(out_ref.dtype)


def on_device(queries, new_kv, pool, block_table, prefix_len, new_slots):
    owners = lax.axis_size("pool")
    half_count = owners // 2
    me = lax.axis_index("pool")
    slot_count, _, kv_heads, page_len, head_dim = pool.shape
    tokens, q_heads, _ = queries.shape
    group = q_heads // kv_heads
    take = block_table.shape[1] // owners // 2
    n_pages = half_count * take
    my_half = me // half_count
    far_half = 1 - my_half

    q_own = queries.reshape(tokens, kv_heads, group, head_dim).transpose(1, 0, 2, 3)
    q_own = q_own.reshape(kv_heads, tokens * group, head_dim)
    q_far = permuted(q_own, half_count)
    q_pair = permuted(q_own, 1)
    q_far_pair = permuted(q_far, 1)

    page_count = (prefix_len + page_len - 1) // page_len
    targets = np.arange(owners, dtype=np.int32)
    first = jnp.asarray(half_of(targets))
    _, send_slots, _ = select_pages(
        jnp.repeat(block_table, 2, axis=0),
        jnp.repeat(page_count, 2, axis=0),
        jnp.full((owners,), me, jnp.int32),
        first,
        take,
        slot_count,
    )
    groups = [list(range(half_count)), list(range(half_count, owners))]

    def exchange(which):
        slots = lax.dynamic_slice_in_dim(send_slots, which * half_count, half_count, 0)
        sent = gather_pages(pool, slots.reshape(-1))
        return lax.all_to_all(
            sent, "pool", split_axis=0, concat_axis=0, tiled=True, axis_index_groups=groups
        )

    pages_far = exchange(far_half)
    pages_near = exchange(my_half)

    holders = my_half * half_count + jnp.arange(half_count, dtype=jnp.int32)

    def valid_keys(device):
        row = lax.dynamic_slice_in_dim(block_table, device // 2, 1, 0)
        length = lax.dynamic_slice_in_dim(prefix_len, device // 2, 1, 0)
        chosen, _, present = select_pages(
            jnp.broadcast_to(row, (half_count, row.shape[1])),
            jnp.broadcast_to((length + page_len - 1) // page_len, (half_count,)),
            holders,
            jnp.broadcast_to(half_of(device), (half_count,)),
            take,
            slot_count,
        )
        left = jnp.clip(length[:, None] - chosen * page_len, 0, page_len)
        return jnp.where(present, left, 0).reshape(-1)

    valid_far = valid_keys(me ^ half_count)
    valid_own = valid_keys(me)
    pair_limit = (1 - half_of(me)) * page_len
    none_causal = jnp.stack([pair_limit, 0 * pair_limit]).astype(jnp.int32)
    valid_pair = jnp.concatenate([valid_own, none_causal])
    valid_own = jnp.concatenate([valid_own, jnp.asarray([page_len, 1], jnp.int32)])
    new_page = new_kv.transpose(1, 2, 0, 3)[None]

    far_pair = attend(valid_far, q_far_pair, pages_far, None, group, "far_pair")
    back_o, back_lse = permuted(far_pair[0], 1), permuted(far_pair[1], 1)
    q_far, _ = lax.optimization_barrier((q_far, far_pair[1]))
    far_own = attend(valid_far, q_far, pages_far, None, group, "far_own")
    far_o, far_lse = combine([far_own, (back_o, back_lse)])
    far_o = far_o.astype(jnp.bfloat16)
    q_pair, far_o, far_lse = lax.optimization_barrier((q_pair, far_o, far_lse))
    home_o = permuted(far_o, half_count)
    home_lse = permuted(far_lse, half_count)

    o_pair, lse_pair = attend(valid_pair, q_pair, pages_near, new_page, group, "near_pair")
    pair_o, pair_lse = permuted(o_pair, 1), permuted(lse_pair, 1)
    q_own, _ = lax.optimization_barrier((q_own, lse_pair))
    o_near, lse_near = attend(valid_own, q_own, pages_near, new_page, group, "near_own")
    attended = pl.pallas_call(
        functools.partial(merge_kernel, group),
        out_shape=jax.ShapeDtypeStruct(queries.shape, queries.dtype),
        compiler_params=pltpu.CompilerParams(vmem_limit_bytes=vmem_bytes),
        name="merge",
    )(o_near, lse_near, pair_o, pair_lse, home_o, home_lse)

    own_slot = lax.dynamic_index_in_dim(new_slots, me, 0, keepdims=False)
    slot = (own_slot % slot_count).reshape(1).astype(jnp.int32)
    updated_pool = write_page(pool, new_page, slot)
    return attended, updated_pool


def solution(mesh):
    placed = (
        P(("groups", "pool"), "head", None),
        P(("groups", "pool"), None, "head", None),
        P(("groups", "pool"), None, "head", None, None),
        P("groups", None),
        P("groups"),
        P("groups"),
    )
    return jax.shard_map(
        on_device,
        mesh=mesh,
        in_specs=placed,
        out_specs=(
            P(("groups", "pool"), "head", None),
            P(("groups", "pool"), None, "head", None, None),
        ),
        check_vma=False,
    )
```

```python
import functools
import math

import jax
import jax.numpy as jnp
import numpy as np
from jax import lax
from jax.experimental import pallas as pl
from jax.experimental.pallas import tpu as pltpu
from jax.sharding import PartitionSpec as P

neg_big = -1e30
vmem_bytes = 32 * 1024 * 1024
lanes = 128
block_rows = 1024
sub_rows = 256
chunk_pages = 16


def permuted(array, apart):
    return lax.ppermute(array, "pool", [(i, i ^ apart) for i in range(lax.axis_size("pool"))])


def half_of(ids):
    return 1 - (ids % 2 ^ ids // 2 % 2)


def select_pages(rows, page_count, holder, first_rank, take, slot_count):
    width = rows.shape[1]
    column = jnp.arange(width, dtype=jnp.int32)
    owned = (
        (rows >= holder[:, None] * slot_count)
        & (rows < (holder[:, None] + 1) * slot_count)
        & (column[None, :] < page_count[:, None])
    )
    before = column[None, :, None] > column[None, None, :]
    rank = jnp.sum((owned[:, None, :] & before).astype(jnp.int32), axis=-1)
    wanted = first_rank[:, None] + 2 * jnp.arange(take, dtype=jnp.int32)[None, :]
    matched = owned[:, None, :] & (rank[:, None, :] == wanted[:, :, None])
    present = jnp.any(matched, axis=-1)
    chosen = jnp.sum(jnp.where(matched, column[None, None, :], 0), axis=-1)
    local = rows - holder[:, None] * slot_count
    slot_id = jnp.sum(jnp.where(matched, local[:, None, :], 0), axis=-1)
    return chosen, slot_id, present


def gather_kernel(slots_ref, pool_ref, out_ref, sems):
    for i in range(out_ref.shape[0]):
        pltpu.make_async_copy(pool_ref.at[slots_ref[i]], out_ref.at[i], sems.at[i]).start()
    for i in range(out_ref.shape[0]):
        pltpu.make_async_copy(pool_ref.at[slots_ref[i]], out_ref.at[i], sems.at[i]).wait()


def gather_pages(pool, slots):
    count = slots.shape[0]
    return pl.pallas_call(
        gather_kernel,
        out_shape=jax.ShapeDtypeStruct((count, *pool.shape[1:]), pool.dtype),
        in_specs=[pl.BlockSpec(memory_space=pltpu.SMEM), pl.BlockSpec(memory_space=pl.ANY)],
        out_specs=pl.BlockSpec(memory_space=pltpu.VMEM),
        scratch_shapes=[pltpu.SemaphoreType.DMA((count,))],
        compiler_params=pltpu.CompilerParams(vmem_limit_bytes=vmem_bytes),
        cost_estimate=pl.CostEstimate(
            flops=0, bytes_accessed=2 * count * pool.nbytes // pool.shape[0], transcendentals=0
        ),
        name="gather_pages",
    )(slots, pool)


def attend_kernel(with_recent, chunk, group, valid_ref, bias_ref, q_ref, pages, *refs):
    if with_recent:
        recent, refs = refs[0], refs[1:]
    o_ref, lse_ref, m_ref, l_ref, acc_ref = refs
    n_pages, _, _, page_len, head_dim = pages.shape
    rows = q_ref.shape[1]
    factor = head_dim ** (-0.5) * math.log2(math.e)
    m_ref[...] = jnp.full_like(m_ref, neg_big)
    l_ref[...] = jnp.zeros_like(l_ref)
    acc_ref[...] = jnp.zeros_like(acc_ref)

    def step(keys, values, mask):
        parts = max(rows // sub_rows, 1)
        size = rows // parts
        for part in range(parts):
            at = pl.ds(part * size, size)
            s = lax.dot_general(
                q_ref[0, at], keys, (((1,), (1,)), ((), ())), preferred_element_type=jnp.float32
            )
            s = mask(s, part * size)
            m_old = m_ref[at]
            m_new = jnp.maximum(m_old, jnp.max(s, axis=1, keepdims=True))
            alpha = jnp.exp2((m_old - m_new) * factor)
            top = m_new[:, :1]
            p = jnp.exp2((s - top) * factor)
            sums = functools.reduce(
                jnp.add,
                [p[:, i : i + lanes] for i in range(0, p.shape[1], lanes)],
            )
            m_ref[at] = m_new
            l_ref[at] = l_ref[at] * alpha + sums
            acc_ref[at] = acc_ref[at] * alpha[:, :1] + jnp.dot(
                p.astype(jnp.bfloat16), values, preferred_element_type=jnp.float32
            )

    for begin in range(0, n_pages, chunk):
        counts = [valid_ref[begin + i] for i in range(chunk)]
        least = functools.reduce(jnp.minimum, counts)
        most = functools.reduce(jnp.maximum, counts)
        span = pl.ds(begin, chunk)
        keys = pages.at[span, 0, 0]
        values = pages.at[span, 1, 0]
        shape = (chunk * page_len, head_dim)

        @pl.when(least == page_len)
        def whole():
            step(keys[...].reshape(shape), values[...].reshape(shape), lambda s, start: s)

        @pl.when((least < page_len) & (most > 0))
        def partly():
            offset = bias_ref[:, pl.ds(begin * page_len, chunk * page_len)]
            step(keys[...].reshape(shape), values[...].reshape(shape), lambda s, start: s + offset)

    if with_recent:
        limit = valid_ref[n_pages]
        causal = valid_ref[n_pages + 1]

        def seen(s, start):
            key_at = lax.broadcasted_iota(jnp.int32, s.shape, 1)
            row_at = lax.broadcasted_iota(jnp.int32, s.shape, 0)
            row_at = row_at + (pl.program_id(1) * rows + start)
            return jnp.where(
                (key_at < limit) & (key_at * group * causal <= row_at), s, 2 * neg_big
            )

        step(recent[0, 0, 0], recent[0, 1, 0], seen)

    total = jnp.maximum(jnp.sum(l_ref[...], axis=1, keepdims=True), 1e-30)
    o_ref[0] = (acc_ref[...] / total).T.astype(o_ref.dtype)
    lse = m_ref[...] * factor + jnp.log2(total)
    lse_ref[0] = lse.T[:1]


def attend(valid, q, pages, recent, group, name):
    kv_heads, n_rows, head_dim = q.shape
    n_pages, _, _, page_len, _ = pages.shape
    rows = math.gcd(n_rows, block_rows)
    chunk = math.gcd(n_pages, chunk_pages)
    page_block = lambda count: pl.BlockSpec(
        (count, 2, 1, page_len, head_dim), lambda k, b: (0, 0, k, 0, 0)
    )
    seen = jnp.arange(page_len)[None, :] < valid[:n_pages, None]
    bias = jnp.where(seen, 0.0, 2 * neg_big).astype(jnp.float32).reshape(1, n_pages * page_len)
    operands = (valid, bias, q, pages) + (() if recent is None else (recent,))
    work = kv_heads * n_rows * n_pages * page_len
    return pl.pallas_call(
        functools.partial(attend_kernel, recent is not None, chunk, group),
        grid=(kv_heads, n_rows // rows),
        out_shape=(
            jax.ShapeDtypeStruct((kv_heads, head_dim, n_rows), jnp.bfloat16),
            jax.ShapeDtypeStruct((kv_heads, 1, n_rows), jnp.float32),
        ),
        in_specs=[
            pl.BlockSpec(memory_space=pltpu.SMEM),
            pl.BlockSpec(bias.shape, lambda k, b: (0, 0)),
            pl.BlockSpec((1, rows, head_dim), lambda k, b: (k, b, 0)),
            page_block(n_pages),
        ]
        + ([] if recent is None else [page_block(1)]),
        out_specs=(
            pl.BlockSpec((1, head_dim, rows), lambda k, b: (k, 0, b)),
            pl.BlockSpec((1, 1, rows), lambda k, b: (k, 0, b)),
        ),
        scratch_shapes=[
            pltpu.VMEM((rows, lanes), jnp.float32),
            pltpu.VMEM((rows, lanes), jnp.float32),
            pltpu.VMEM((rows, head_dim), jnp.float32),
        ],
        compiler_params=pltpu.CompilerParams(vmem_limit_bytes=vmem_bytes),
        cost_estimate=pl.CostEstimate(
            flops=4 * work * head_dim, bytes_accessed=4 * 2**20, transcendentals=work
        ),
        name=name,
    )(*operands)


def write_kernel(slot_ref, pool_ref, page_ref, out_ref):
    out_ref[...] = pool_ref[...]
    count = out_ref.shape[0]
    at = slot_ref[0] - pl.program_id(0) * count
    for i in range(count):

        @pl.when(at == i)
        def put():
            out_ref[i] = page_ref[0]


def write_page(pool, page, slot):
    slot_count = pool.shape[0]
    count = max(i for i in range(1, 5) if slot_count % i == 0)
    block = (count, *pool.shape[1:])
    return pl.pallas_call(
        write_kernel,
        grid=(slot_count // count,),
        out_shape=jax.ShapeDtypeStruct(pool.shape, pool.dtype),
        in_specs=[
            pl.BlockSpec(memory_space=pltpu.SMEM),
            pl.BlockSpec(block, lambda i: (i, 0, 0, 0, 0)),
            pl.BlockSpec(page.shape, lambda i: (0, 0, 0, 0, 0)),
        ],
        out_specs=pl.BlockSpec(block, lambda i: (i, 0, 0, 0, 0)),
        compiler_params=pltpu.CompilerParams(vmem_limit_bytes=vmem_bytes),
        cost_estimate=pl.CostEstimate(flops=0, bytes_accessed=2 * pool.nbytes, transcendentals=0),
        name="write_page",
    )(slot, pool, page)


def combine(parts):
    top = functools.reduce(jnp.maximum, [lse for _, lse in parts])
    weights = [jnp.exp2(lse - top) for _, lse in parts]
    total = functools.reduce(jnp.add, weights)
    mixed = functools.reduce(
        jnp.add, [o.astype(jnp.float32) * w for (o, _), w in zip(parts, weights)]
    )
    return mixed / total, top + jnp.log2(total)


def merge_kernel(group, *refs):
    out_ref = refs[-1]
    parts = [(refs[2 * i], refs[2 * i + 1]) for i in range(len(refs) // 2)]
    tokens = out_ref.shape[0]
    heads = []
    for k in range(parts[0][0].shape[0]):
        mixed, _ = combine([(o[k], lse[k]) for o, lse in parts])
        heads.append(mixed.T.reshape(tokens, group, mixed.shape[0]))
    out_ref[...] = jnp.concatenate(heads, axis=1).astype(out_ref.dtype)


def on_device(queries, new_kv, pool, block_table, prefix_len, new_slots):
    owners = lax.axis_size("pool")
    half_count = owners // 2
    me = lax.axis_index("pool")
    slot_count, _, kv_heads, page_len, head_dim = pool.shape
    tokens, q_heads, _ = queries.shape
    group = q_heads // kv_heads
    take = block_table.shape[1] // owners // 2
    n_pages = half_count * take
    my_half = me // half_count
    far_half = 1 - my_half

    q_own = queries.reshape(tokens, kv_heads, group, head_dim).transpose(1, 0, 2, 3)
    q_own = q_own.reshape(kv_heads, tokens * group, head_dim)
    q_far = permuted(q_own, half_count)
    q_pair = permuted(q_own, 1)
    q_far_pair = permuted(q_own, half_count ^ 1)

    page_count = (prefix_len + page_len - 1) // page_len
    targets = np.arange(owners, dtype=np.int32)
    first = jnp.asarray(half_of(targets))
    _, send_slots, _ = select_pages(
        jnp.repeat(block_table, 2, axis=0),
        jnp.repeat(page_count, 2, axis=0),
        jnp.full((owners,), me, jnp.int32),
        first,
        take,
        slot_count,
    )
    groups = [list(range(half_count)), list(range(half_count, owners))]

    def exchange(which):
        slots = lax.dynamic_slice_in_dim(send_slots, which * half_count, half_count, 0)
        sent = gather_pages(pool, slots.reshape(-1))
        return lax.all_to_all(
            sent, "pool", split_axis=0, concat_axis=0, tiled=True, axis_index_groups=groups
        )

    pages_far = exchange(far_half)
    pages_near = exchange(my_half)

    holders = my_half * half_count + jnp.arange(half_count, dtype=jnp.int32)

    def valid_keys(device):
        row = lax.dynamic_slice_in_dim(block_table, device // 2, 1, 0)
        length = lax.dynamic_slice_in_dim(prefix_len, device // 2, 1, 0)
        chosen, _, present = select_pages(
            jnp.broadcast_to(row, (half_count, row.shape[1])),
            jnp.broadcast_to((length + page_len - 1) // page_len, (half_count,)),
            holders,
            jnp.broadcast_to(half_of(device), (half_count,)),
            take,
            slot_count,
        )
        left = jnp.clip(length[:, None] - chosen * page_len, 0, page_len)
        return jnp.where(present, left, 0).reshape(-1)

    valid_far = valid_keys(me ^ half_count)
    valid_own = valid_keys(me)
    pair_limit = (1 - half_of(me)) * page_len
    none_causal = jnp.stack([pair_limit, 0 * pair_limit]).astype(jnp.int32)
    valid_pair = jnp.concatenate([valid_own, none_causal])
    valid_own = jnp.concatenate([valid_own, jnp.asarray([page_len, 1], jnp.int32)])
    new_page = new_kv.transpose(1, 2, 0, 3)[None]
    own_slot = lax.dynamic_index_in_dim(new_slots, me, 0, keepdims=False)
    slot = (own_slot % slot_count).reshape(1).astype(jnp.int32)
    updated_pool = write_page(pool, new_page, slot)
    valid_far, updated_pool = lax.optimization_barrier((valid_far, updated_pool))

    far_pair = attend(valid_far, q_far_pair, pages_far, None, group, "far_pair")
    back_o, back_lse = permuted(far_pair[0], 1), permuted(far_pair[1], 1)
    q_far, _ = lax.optimization_barrier((q_far, far_pair[1]))
    far_own = attend(valid_far, q_far, pages_far, None, group, "far_own")
    far_o, far_lse = combine([far_own, (back_o, back_lse)])
    far_o = far_o.astype(jnp.bfloat16)
    q_pair, far_o, far_lse = lax.optimization_barrier((q_pair, far_o, far_lse))
    home_o = permuted(far_o, half_count)
    home_lse = permuted(far_lse, half_count)

    o_pair, lse_pair = attend(valid_pair, q_pair, pages_near, new_page, group, "near_pair")
    pair_o, pair_lse = permuted(o_pair, 1), permuted(lse_pair, 1)
    q_own, _ = lax.optimization_barrier((q_own, lse_pair))
    o_near, lse_near = attend(valid_own, q_own, pages_near, new_page, group, "near_own")
    attended = pl.pallas_call(
        functools.partial(merge_kernel, group),
        out_shape=jax.ShapeDtypeStruct(queries.shape, queries.dtype),
        compiler_params=pltpu.CompilerParams(vmem_limit_bytes=vmem_bytes),
        name="merge",
    )(o_near, lse_near, pair_o, pair_lse, home_o, home_lse)
    return attended, updated_pool


def solution(mesh):
    placed = (
        P(("groups", "pool"), "head", None),
        P(("groups", "pool"), None, "head", None),
        P(("groups", "pool"), None, "head", None, None),
        P("groups", None),
        P("groups"),
        P("groups"),
    )
    return jax.shard_map(
        on_device,
        mesh=mesh,
        in_specs=placed,
        out_specs=(
            P(("groups", "pool"), "head", None),
            P(("groups", "pool"), None, "head", None, None),
        ),
        check_vma=False,
    )
```

```python
import functools
import math

import jax
import jax.numpy as jnp
import numpy as np
from jax import lax
from jax.experimental import pallas as pl
from jax.experimental.pallas import tpu as pltpu
from jax.sharding import PartitionSpec as P

neg_big = -1e30
vmem_bytes = 32 * 1024 * 1024
lanes = 128
block_rows = 1024
sub_rows = 256
chunk_pages = 16


def permuted(array, apart):
    return lax.ppermute(array, "pool", [(i, i ^ apart) for i in range(lax.axis_size("pool"))])


def half_of(ids):
    return 1 - (ids % 2 ^ ids // 2 % 2)


def select_pages(rows, page_count, holder, first_rank, take, slot_count):
    width = rows.shape[1]
    column = jnp.arange(width, dtype=jnp.int32)
    owned = (
        (rows >= holder[:, None] * slot_count)
        & (rows < (holder[:, None] + 1) * slot_count)
        & (column[None, :] < page_count[:, None])
    )
    before = column[None, :, None] > column[None, None, :]
    rank = jnp.sum((owned[:, None, :] & before).astype(jnp.int32), axis=-1)
    wanted = first_rank[:, None] + 2 * jnp.arange(take, dtype=jnp.int32)[None, :]
    matched = owned[:, None, :] & (rank[:, None, :] == wanted[:, :, None])
    present = jnp.any(matched, axis=-1)
    chosen = jnp.sum(jnp.where(matched, column[None, None, :], 0), axis=-1)
    local = rows - holder[:, None] * slot_count
    slot_id = jnp.sum(jnp.where(matched, local[:, None, :], 0), axis=-1)
    return chosen, slot_id, present


def gather_kernel(slots_ref, pool_ref, out_ref, sems):
    for i in range(out_ref.shape[0]):
        pltpu.make_async_copy(pool_ref.at[slots_ref[i]], out_ref.at[i], sems.at[i]).start()
    for i in range(out_ref.shape[0]):
        pltpu.make_async_copy(pool_ref.at[slots_ref[i]], out_ref.at[i], sems.at[i]).wait()


def gather_pages(pool, slots):
    count = slots.shape[0]
    return pl.pallas_call(
        gather_kernel,
        out_shape=jax.ShapeDtypeStruct((count, *pool.shape[1:]), pool.dtype),
        in_specs=[pl.BlockSpec(memory_space=pltpu.SMEM), pl.BlockSpec(memory_space=pl.ANY)],
        out_specs=pl.BlockSpec(memory_space=pltpu.VMEM),
        scratch_shapes=[pltpu.SemaphoreType.DMA((count,))],
        compiler_params=pltpu.CompilerParams(vmem_limit_bytes=vmem_bytes),
        cost_estimate=pl.CostEstimate(
            flops=0, bytes_accessed=2 * count * pool.nbytes // pool.shape[0], transcendentals=0
        ),
        name="gather_pages",
    )(slots, pool)


def attend_kernel(with_recent, chunk, group, valid_ref, bias_ref, q_ref, pages, *refs):
    if with_recent:
        recent, refs = refs[0], refs[1:]
    o_ref, lse_ref, m_ref, l_ref, acc_ref = refs
    n_pages, _, _, page_len, head_dim = pages.shape
    rows = q_ref.shape[1]
    factor = head_dim ** (-0.5) * math.log2(math.e)
    m_ref[...] = jnp.full_like(m_ref, neg_big)
    l_ref[...] = jnp.zeros_like(l_ref)
    acc_ref[...] = jnp.zeros_like(acc_ref)

    def step(keys, values, mask):
        parts = max(rows // sub_rows, 1)
        size = rows // parts
        for part in range(parts):
            at = pl.ds(part * size, size)
            s = lax.dot_general(
                q_ref[0, at], keys, (((1,), (1,)), ((), ())), preferred_element_type=jnp.float32
            )
            s = mask(s, part * size)
            m_old = m_ref[at]
            m_new = jnp.maximum(m_old, jnp.max(s, axis=1, keepdims=True))
            alpha = jnp.exp2((m_old - m_new) * factor)
            top = m_new[:, :1]
            p = jnp.exp2((s - top) * factor)
            sums = functools.reduce(
                jnp.add,
                [p[:, i : i + lanes] for i in range(0, p.shape[1], lanes)],
            )
            m_ref[at] = m_new
            l_ref[at] = l_ref[at] * alpha + sums
            acc_ref[at] = acc_ref[at] * alpha[:, :1] + jnp.dot(
                p.astype(jnp.bfloat16), values, preferred_element_type=jnp.float32
            )

    for begin in range(0, n_pages, chunk):
        counts = [valid_ref[begin + i] for i in range(chunk)]
        least = functools.reduce(jnp.minimum, counts)
        most = functools.reduce(jnp.maximum, counts)
        span = pl.ds(begin, chunk)
        keys = pages.at[span, 0, 0]
        values = pages.at[span, 1, 0]
        shape = (chunk * page_len, head_dim)

        @pl.when(least == page_len)
        def whole():
            step(keys[...].reshape(shape), values[...].reshape(shape), lambda s, start: s)

        @pl.when((least < page_len) & (most > 0))
        def partly():
            offset = bias_ref[:, pl.ds(begin * page_len, chunk * page_len)]
            step(keys[...].reshape(shape), values[...].reshape(shape), lambda s, start: s + offset)

    if with_recent:
        limit = valid_ref[n_pages]
        causal = valid_ref[n_pages + 1]

        def seen(s, start):
            key_at = lax.broadcasted_iota(jnp.int32, s.shape, 1)
            row_at = lax.broadcasted_iota(jnp.int32, s.shape, 0)
            row_at = row_at + (pl.program_id(1) * rows + start)
            return jnp.where(
                (key_at < limit) & (key_at * group * causal <= row_at), s, 2 * neg_big
            )

        step(recent[0, 0, 0], recent[0, 1, 0], seen)

    total = jnp.maximum(jnp.sum(l_ref[...], axis=1, keepdims=True), 1e-30)
    o_ref[0] = (acc_ref[...] / total).T.astype(o_ref.dtype)
    lse = m_ref[...] * factor + jnp.log2(total)
    lse_ref[0] = lse.T[:1]


def attend(valid, q, pages, recent, group, name):
    kv_heads, n_rows, head_dim = q.shape
    n_pages, _, _, page_len, _ = pages.shape
    rows = math.gcd(n_rows, block_rows)
    chunk = math.gcd(n_pages, chunk_pages)
    page_block = lambda count: pl.BlockSpec(
        (count, 2, 1, page_len, head_dim), lambda k, b: (0, 0, k, 0, 0)
    )
    seen = jnp.arange(page_len)[None, :] < valid[:n_pages, None]
    bias = jnp.where(seen, 0.0, 2 * neg_big).astype(jnp.float32).reshape(1, n_pages * page_len)
    operands = (valid, bias, q, pages) + (() if recent is None else (recent,))
    work = kv_heads * n_rows * n_pages * page_len
    return pl.pallas_call(
        functools.partial(attend_kernel, recent is not None, chunk, group),
        grid=(kv_heads, n_rows // rows),
        out_shape=(
            jax.ShapeDtypeStruct((kv_heads, head_dim, n_rows), jnp.bfloat16),
            jax.ShapeDtypeStruct((kv_heads, 1, n_rows), jnp.float32),
        ),
        in_specs=[
            pl.BlockSpec(memory_space=pltpu.SMEM),
            pl.BlockSpec(bias.shape, lambda k, b: (0, 0)),
            pl.BlockSpec((1, rows, head_dim), lambda k, b: (k, b, 0)),
            page_block(n_pages),
        ]
        + ([] if recent is None else [page_block(1)]),
        out_specs=(
            pl.BlockSpec((1, head_dim, rows), lambda k, b: (k, 0, b)),
            pl.BlockSpec((1, 1, rows), lambda k, b: (k, 0, b)),
        ),
        scratch_shapes=[
            pltpu.VMEM((rows, lanes), jnp.float32),
            pltpu.VMEM((rows, lanes), jnp.float32),
            pltpu.VMEM((rows, head_dim), jnp.float32),
        ],
        compiler_params=pltpu.CompilerParams(vmem_limit_bytes=vmem_bytes),
        cost_estimate=pl.CostEstimate(
            flops=4 * work * head_dim, bytes_accessed=4 * 2**20, transcendentals=work
        ),
        name=name,
    )(*operands)


def write_kernel(slot_ref, pool_ref, page_ref, out_ref):
    out_ref[...] = pool_ref[...]
    count = out_ref.shape[0]
    at = slot_ref[0] - pl.program_id(0) * count
    for i in range(count):

        @pl.when(at == i)
        def put():
            out_ref[i] = page_ref[0]


def write_page(pool, page, slot):
    slot_count = pool.shape[0]
    count = max(i for i in range(1, 5) if slot_count % i == 0)
    block = (count, *pool.shape[1:])
    return pl.pallas_call(
        write_kernel,
        grid=(slot_count // count,),
        out_shape=jax.ShapeDtypeStruct(pool.shape, pool.dtype),
        in_specs=[
            pl.BlockSpec(memory_space=pltpu.SMEM),
            pl.BlockSpec(block, lambda i: (i, 0, 0, 0, 0)),
            pl.BlockSpec(page.shape, lambda i: (0, 0, 0, 0, 0)),
        ],
        out_specs=pl.BlockSpec(block, lambda i: (i, 0, 0, 0, 0)),
        compiler_params=pltpu.CompilerParams(vmem_limit_bytes=vmem_bytes),
        cost_estimate=pl.CostEstimate(flops=0, bytes_accessed=2 * pool.nbytes, transcendentals=0),
        name="write_page",
    )(slot, pool, page)


def combine(parts):
    top = functools.reduce(jnp.maximum, [lse for _, lse in parts])
    weights = [jnp.exp2(lse - top) for _, lse in parts]
    total = functools.reduce(jnp.add, weights)
    mixed = functools.reduce(
        jnp.add, [o.astype(jnp.float32) * w for (o, _), w in zip(parts, weights)]
    )
    return mixed / total, top + jnp.log2(total)


def merge_kernel(group, *refs):
    out_ref = refs[-1]
    parts = [(refs[2 * i], refs[2 * i + 1]) for i in range(len(refs) // 2)]
    tokens = out_ref.shape[0]
    heads = []
    for k in range(parts[0][0].shape[0]):
        mixed, _ = combine([(o[k], lse[k]) for o, lse in parts])
        heads.append(mixed.T.reshape(tokens, group, mixed.shape[0]))
    out_ref[...] = jnp.concatenate(heads, axis=1).astype(out_ref.dtype)


def on_device(queries, new_kv, pool, block_table, prefix_len, new_slots):
    owners = lax.axis_size("pool")
    half_count = owners // 2
    me = lax.axis_index("pool")
    slot_count, _, kv_heads, page_len, head_dim = pool.shape
    tokens, q_heads, _ = queries.shape
    group = q_heads // kv_heads
    take = block_table.shape[1] // owners // 2
    n_pages = half_count * take
    my_half = me // half_count
    far_half = 1 - my_half

    q_own = queries.reshape(tokens, kv_heads, group, head_dim).transpose(1, 0, 2, 3)
    q_own = q_own.reshape(kv_heads, tokens * group, head_dim)
    q_far = permuted(q_own, half_count)
    q_pair = permuted(q_own, 1)
    q_far_pair = permuted(q_own, half_count ^ 1)

    page_count = (prefix_len + page_len - 1) // page_len
    targets = np.arange(owners, dtype=np.int32)
    first = jnp.asarray(half_of(targets))
    _, send_slots, _ = select_pages(
        jnp.repeat(block_table, 2, axis=0),
        jnp.repeat(page_count, 2, axis=0),
        jnp.full((owners,), me, jnp.int32),
        first,
        take,
        slot_count,
    )
    groups = [list(range(half_count)), list(range(half_count, owners))]

    def exchange(all_slots, which):
        slots = lax.dynamic_slice_in_dim(all_slots, which * half_count, half_count, 0)
        sent = gather_pages(pool, slots.reshape(-1))
        return lax.all_to_all(
            sent, "pool", split_axis=0, concat_axis=0, tiled=True, axis_index_groups=groups
        )

    pages_far = exchange(send_slots, far_half)
    new_page = new_kv.transpose(1, 2, 0, 3)[None]
    own_slot = lax.dynamic_index_in_dim(new_slots, me, 0, keepdims=False)
    slot = (own_slot % slot_count).reshape(1).astype(jnp.int32)
    updated_pool = write_page(pool, new_page, slot)
    send_slots, updated_pool = lax.optimization_barrier((send_slots, updated_pool))
    pages_near = exchange(send_slots, my_half)

    holders = my_half * half_count + jnp.arange(half_count, dtype=jnp.int32)

    def valid_keys(device):
        row = lax.dynamic_slice_in_dim(block_table, device // 2, 1, 0)
        length = lax.dynamic_slice_in_dim(prefix_len, device // 2, 1, 0)
        chosen, _, present = select_pages(
            jnp.broadcast_to(row, (half_count, row.shape[1])),
            jnp.broadcast_to((length + page_len - 1) // page_len, (half_count,)),
            holders,
            jnp.broadcast_to(half_of(device), (half_count,)),
            take,
            slot_count,
        )
        left = jnp.clip(length[:, None] - chosen * page_len, 0, page_len)
        return jnp.where(present, left, 0).reshape(-1)

    valid_far = valid_keys(me ^ half_count)
    valid_own = valid_keys(me)
    pair_limit = (1 - half_of(me)) * page_len
    none_causal = jnp.stack([pair_limit, 0 * pair_limit]).astype(jnp.int32)
    valid_pair = jnp.concatenate([valid_own, none_causal])
    valid_own = jnp.concatenate([valid_own, jnp.asarray([page_len, 1], jnp.int32)])
    far_pair = attend(valid_far, q_far_pair, pages_far, None, group, "far_pair")
    back_o, back_lse = permuted(far_pair[0], 1), permuted(far_pair[1], 1)
    q_far, _ = lax.optimization_barrier((q_far, far_pair[1]))
    far_own = attend(valid_far, q_far, pages_far, None, group, "far_own")
    far_o, far_lse = combine([far_own, (back_o, back_lse)])
    far_o = far_o.astype(jnp.bfloat16)
    q_pair, far_o, far_lse = lax.optimization_barrier((q_pair, far_o, far_lse))
    home_o = permuted(far_o, half_count)
    home_lse = permuted(far_lse, half_count)

    o_pair, lse_pair = attend(valid_pair, q_pair, pages_near, new_page, group, "near_pair")
    pair_o, pair_lse = permuted(o_pair, 1), permuted(lse_pair, 1)
    q_own, _ = lax.optimization_barrier((q_own, lse_pair))
    o_near, lse_near = attend(valid_own, q_own, pages_near, new_page, group, "near_own")
    attended = pl.pallas_call(
        functools.partial(merge_kernel, group),
        out_shape=jax.ShapeDtypeStruct(queries.shape, queries.dtype),
        compiler_params=pltpu.CompilerParams(vmem_limit_bytes=vmem_bytes),
        name="merge",
    )(o_near, lse_near, pair_o, pair_lse, home_o, home_lse)
    return attended, updated_pool


def solution(mesh):
    placed = (
        P(("groups", "pool"), "head", None),
        P(("groups", "pool"), None, "head", None),
        P(("groups", "pool"), None, "head", None, None),
        P("groups", None),
        P("groups"),
        P("groups"),
    )
    return jax.shard_map(
        on_device,
        mesh=mesh,
        in_specs=placed,
        out_specs=(
            P(("groups", "pool"), "head", None),
            P(("groups", "pool"), None, "head", None, None),
        ),
        check_vma=False,
    )
```
